256 devices in a mesh: seq: 32 (over y_lo, z, core), ulysses: 8 (over y_hi, x).
Axes of the slice: x: 4, y: 4 (y_hi: 2, y_lo: 2; y = y_hi * 2 + y_lo), z: 8, core: 2. Of those that a mesh axis runs over, the one named last changes fastest.
Arguments:
- queries: bfloat16 [8192, 3072], P(('seq', 'ulysses')), may hold values from -90 to 90
- keys_edit: bfloat16 [8192, 3072], P(('seq', 'ulysses')), may hold values from -6 to 6
- values_edit: bfloat16 [8192, 3072], P(('seq', 'ulysses')), may hold values from -6 to 6
- keys_source: bfloat16 [8192, 3072], P(('seq', 'ulysses')), may hold values from -6 to 6
- values_source: bfloat16 [8192, 3072], P(('seq', 'ulysses')), may hold values from -6 to 6
- edit_mask: int32 [8192], P('seq'), may hold values 0 or 1
- inject_gate: float32 [50, 24], replicated, may hold values from 0 to 0.9
- step_index: int32 [1], replicated, may hold values from 0 to 49
Outputs:
- attended: bfloat16 [8192, 3072], P(('seq', 'ulysses'))
The draws below stay inside these ranges and needn't reach their ends.
All inputs are finite; a program needn't handle non-finite values. No bound on the sum of `edit_mask` on one device may be relied on, other than what follows from the above.
Results may differ from the reference program's by a relative error of at most 0.008.
Values may be sent and summed in bfloat16 or wider, within the bound.
No kernel may reach another device: no remote copies, remote signals or barrier semaphores. Data moves between devices by JAX's collectives and lax.ppermute only.
A program may use at most 128 MiB of HBM per device.

```python
import jax
import jax.numpy as jnp
from jax import lax

HEADS = 24
HEAD_DIM = 128
STEPS = 50
TOKENS = 8192
FEATURES = 3072


def drawn_keys(key, number):
    key = jax.random.fold_in(key, number)
    bulk = jnp.clip(jax.random.normal(key, (TOKENS, FEATURES), jnp.float32), -6.0, 6.0)
    return jnp.clip(bulk, -6.0, 6.0).astype(jnp.bfloat16)


def draw_queries(key, part):
    key = jax.random.fold_in(key, 11)
    bulk = jnp.clip(2.5 * jax.random.normal(key, (TOKENS, FEATURES), jnp.float32), -15.0, 15.0)
    return bulk.astype(jnp.bfloat16)


def draw_keys_edit(key, part):
    return drawn_keys(key, 23)


def draw_keys_source(key, part):
    return drawn_keys(key, 37)


def place_ends(array, stream_key, least, high):
    index_at = [jax.random.randint(jax.random.fold_in(stream_key, axis), (), 0, length) for axis, length in enumerate(array.shape)]
    longest = array.shape.index(max(array.shape))
    neighbour = index_at[:longest] + [(index_at[longest] + 1) % array.shape[longest]] + index_at[longest + 1:]
    return array.at[tuple(index_at)].set(least).at[tuple(neighbour)].set(high)


def steps_of(key, dims, pieces, low, top_value):
    gain, own = 1.0, jax.random.fold_in(key, 6)
    for axis_at, parts in pieces:
        heights = jnp.exp(jax.random.uniform(jax.random.fold_in(own, axis_at), (parts,), jnp.float32, low / len(pieces), top_value / len(pieces)))
        gain = gain * jnp.repeat(heights, dims[axis_at] // parts).reshape([-1 if axis == axis_at else 1 for axis in range(len(dims))])
    return gain


def gaussian(own_key, extent, scale, reach, split=(), kind=jnp.bfloat16):
    array = jax.random.normal(own_key, extent, jnp.float32) * scale
    if len(split) > 0:
        array = steps_of(own_key, extent, split, -0.22, 0.18) * array
    return jnp.clip(array, min=-reach, max=reach).astype(kind)


def setup_inputs(seed: int = 0) -> dict:
    seeds = jax.random.split(jax.random.key(seed), 9)
    queries = draw_queries(jax.random.fold_in(seeds[8], 71), 0)
    keys_edit = draw_keys_edit(jax.random.fold_in(seeds[8], 71), 0)
    values_edit = gaussian(seeds[2], (TOKENS, FEATURES), 1.0, 6.0, ((0, 256),))
    keys_source = draw_keys_source(jax.random.fold_in(seeds[8], 71), 0)
    values_source = gaussian(seeds[4], (TOKENS, FEATURES), 1.0, 6.0, ((0, 256),))
    edit_mask = place_ends((jax.random.randint(seeds[5], (TOKENS,), 0, 3) < 1).astype(jnp.int32), jax.random.fold_in(seeds[5], 1), 0, 1)
    inject_gate = jnp.clip(jax.random.uniform(seeds[6], (STEPS, HEADS), jnp.float32, 0.0, 0.9), 0.0, 0.9)
    step_index = jax.random.randint(seeds[7], (1,), 0, STEPS).astype(jnp.int32)
    return dict(queries=queries, keys_edit=keys_edit, values_edit=values_edit, keys_source=keys_source, values_source=values_source, edit_mask=edit_mask, inject_gate=inject_gate, step_index=step_index)


def mix_pair(edit, source, flags, strength):
    edit_f = edit.astype(jnp.float32)
    source_f = source.astype(jnp.float32)
    mixed = jnp.where(flags[:, None] == 1, edit_f, source_f + strength[None, :] * (edit_f - source_f))
    return mixed.astype(jnp.bfloat16)


def reference(queries, keys_edit, values_edit, keys_source, values_source, edit_mask, inject_gate, step_index):
    picked = (jnp.arange(STEPS, dtype=jnp.int32) == step_index[0]).astype(jnp.float32)
    head_gate = jnp.dot(picked, inject_gate, precision=lax.Precision.HIGHEST)
    strength = jnp.repeat(head_gate, HEAD_DIM)
    mixed_keys = mix_pair(keys_edit, keys_source, edit_mask, strength)
    mixed_values = mix_pair(values_edit, values_source, edit_mask, strength)
    key_heads = mixed_keys.astype(jnp.float32).reshape(TOKENS, HEADS, HEAD_DIM)
    value_heads = mixed_values.astype(jnp.float32).reshape(TOKENS, HEADS, HEAD_DIM)
    block_rows = min(256, TOKENS)
    query_blocks = queries.reshape(TOKENS // block_rows, block_rows, HEADS, HEAD_DIM)
    scale = HEAD_DIM ** -0.5

    def one_block(query_block):
        scores = jnp.einsum("qhd,khd->hqk", query_block.astype(jnp.float32), key_heads) * scale
        top = jnp.max(scores, axis=-1, keepdims=True)
        expo = jnp.exp(scores - top)
        totals = jnp.sum(expo, axis=-1)
        weights = expo.astype(jnp.bfloat16).astype(jnp.float32)
        summed = jnp.einsum("hqk,khd->qhd", weights, value_heads)
        return (summed / totals.T[:, :, None]).astype(jnp.bfloat16)

    attended = lax.map(one_block, query_blocks)
    return attended.reshape(TOKENS, FEATURES)
```

```python
import functools

import jax
import jax.numpy as jnp
from jax import lax
from jax.experimental import pallas as pl
from jax.experimental.pallas import tpu as pltpu
from jax.sharding import PartitionSpec as P

NX, NY, NZ = 4, 4, 8
HEAD = 128
TOK = 32
GROUP_HEADS = 6
CHUNKS = 1
WIDTH = GROUP_HEADS * HEAD // CHUNKS
CH_HEADS = GROUP_HEADS // CHUNKS
LOG2E = 1.4426950408889634
SCALE2 = HEAD**-0.5 * LOG2E
VMEM = 48 * 1024 * 1024


def coords(index):
    seq, uly = divmod(index, 8)
    core = seq % 2
    z = (seq // 2) % NZ
    y = 2 * (uly // NX) + seq // (2 * NZ)
    return uly % NX, y, z, core


def index_of(x, y, z, core):
    return (((y % 2) * NZ + z) * 2 + core) * 8 + (y // 2) * NX + x


def permute(value, move):
    pairs = [(i, index_of(*move(*coords(i)))) for i in range(2 * NX * NY * NZ)]
    return lax.ppermute(value, ("seq", "ulysses"), pairs)


def shift_x(value, d):
    return permute(value, lambda x, y, z, c: ((x + d) % NX, y, z, c))


def shift_y(value, d):
    return permute(value, lambda x, y, z, c: (x, (y + d) % NY, z, c))


def ring_z(value):
    return permute(value, lambda x, y, z, c: (x, y, (z + 1 - 2 * c) % NZ, c))


def swap_core(value):
    return permute(value, lambda x, y, z, c: (x, y, z, 1 - c))


def cost(flops, nbytes, trans=0):
    return pl.CostEstimate(flops=int(flops), bytes_accessed=int(nbytes), transcendentals=int(trans))


def params():
    return pltpu.CompilerParams(vmem_limit_bytes=VMEM)


def mix_kernel(where_ref, step_ref, q_ref, ke_ref, ve_ref, ks_ref, vs_ref, mask_ref, gate_ref, *outs):
    y, u = where_ref[0], where_ref[1]
    lane = lax.broadcasted_iota(jnp.int32, (TOK, 256), 1)
    row = lax.broadcasted_iota(jnp.int32, (TOK, 256), 0)
    picked = jnp.where(lane == u * TOK + row, jnp.broadcast_to(mask_ref[...], (TOK, 256)), 0)
    inside = jnp.sum(picked, axis=1, keepdims=True) == 1
    gates = gate_ref[pl.ds(step_ref[0], 1), :]
    head_lane = lax.broadcasted_iota(jnp.int32, gates.shape, 1)
    for d in range(NY):
        group = lax.rem(y + d, NY)
        for c in range(CHUNKS):
            out = outs[c * NY + d]
            for h in range(CH_HEADS):
                head = group * GROUP_HEADS + c * CH_HEADS + h
                strength = jnp.sum(jnp.where(head_lane == head, gates, 0.0), axis=1, keepdims=True)
                cols = pl.ds(pl.multiple_of(head * HEAD, HEAD), HEAD)
                to = slice(h * HEAD, (h + 1) * HEAD)
                for n, (edit, source) in enumerate(((ke_ref, ks_ref), (ve_ref, vs_ref))):
                    e = edit[:, cols].astype(jnp.float32)
                    s = source[:, cols].astype(jnp.float32)
                    mixed = jnp.where(inside, e, s + strength * (e - s))
                    out[n * TOK : (n + 1) * TOK, to] = mixed.astype(jnp.bfloat16)
                out[2 * TOK : 3 * TOK, to] = q_ref[:, cols]


def mix(where, step_index, queries, ke, ve, ks, vs, edit_mask, gate):
    vmem = pl.BlockSpec(memory_space=pltpu.VMEM)
    smem = pl.BlockSpec(memory_space=pltpu.SMEM)
    return pl.pallas_call(
        mix_kernel,
        out_shape=[jax.ShapeDtypeStruct((3 * TOK, WIDTH), jnp.bfloat16)] * (NY * CHUNKS),
        in_specs=[smem, smem] + [vmem] * 7,
        out_specs=[vmem] * (NY * CHUNKS),
        compiler_params=params(),
        cost_estimate=cost(1e6, 2e6),
        name="mix",
    )(where, step_index, queries, ke, ve, ks, vs, edit_mask.reshape(1, -1), gate)


def flash_kernel(first, last, blocks, *refs):
    refs = list(refs)
    q_refs, refs = refs[:NX], refs[NX:]
    kv_refs, refs = refs[:blocks], refs[blocks:]
    if not first:
        acc_in, ml_in, refs = refs[0], refs[1], refs[2:]
    rows = q_refs[0].shape[0]
    half = kv_refs[0].shape[0] // 2
    keys = jnp.concatenate([r[:half, :] for r in kv_refs], axis=0)
    values = jnp.concatenate([r[half:, :] for r in kv_refs], axis=0)
    span = 2 * rows
    for part in range(NX // 2):
        at = slice(part * span, (part + 1) * span)
        q = jnp.concatenate([q_refs[2 * part][...], q_refs[2 * part + 1][...]], axis=0)
        s = lax.dot_general(keys, q, (((1,), (1,)), ((), ())), preferred_element_type=jnp.float32)
        top = jnp.max(s, axis=0, keepdims=True)
        if not first:
            old = ml_in[0:1, at]
            top = jnp.maximum(top, old)
        p = jnp.exp2((s - top) * SCALE2)
        total = jnp.sum(p, axis=0, keepdims=True)
        o = lax.dot_general(
            values, p.astype(jnp.bfloat16), (((0,), (0,)), ((), ())), preferred_element_type=jnp.float32
        )
        if not first:
            alpha = jnp.exp2((old - top) * SCALE2)
            total = total + alpha * ml_in[1:2, at]
            o = o + alpha * acc_in[:, at]
        if last:
            o = o / total
            lse = top * SCALE2 + jnp.log2(total)
            hi = lse.astype(jnp.bfloat16).astype(jnp.float32)
            mid = (lse - hi).astype(jnp.bfloat16).astype(jnp.float32)
            low = lse - hi - mid
            r = lax.broadcasted_iota(jnp.int32, (16, span), 0)
            tail = jnp.where(r == 0, hi, jnp.where(r == 1, mid, jnp.where(r == 2, low, 0.0)))
            for i in range(2):
                out = refs[2 * part + i]
                cut = slice(i * rows, (i + 1) * rows)
                out[:HEAD, :] = o[:, cut].astype(jnp.bfloat16)
                out[HEAD:, :] = tail[:, cut].astype(jnp.bfloat16)
        else:
            refs[0][:, at] = o
            refs[1][0:1, at] = top
            refs[1][1:2, at] = total


def flash(q_parts, kv_blocks, state, last):
    rows = q_parts[0].shape[0]
    width = q_parts[0].shape[1]
    heads = width // HEAD
    queries = NX * rows
    first = state is None
    col = lambda n: pl.BlockSpec((n, HEAD), lambda h: (0, h))
    state_specs = [
        pl.BlockSpec((HEAD, queries), lambda h: (h, 0)),
        pl.BlockSpec((8, queries), lambda h: (h, 0)),
    ]
    in_specs = [col(rows)] * NX + [col(b.shape[0]) for b in kv_blocks]
    if last:
        out_shape = [jax.ShapeDtypeStruct((HEAD + 16, heads * rows), jnp.bfloat16)] * NX
        out_specs = [pl.BlockSpec((HEAD + 16, rows), lambda h: (0, h))] * NX
    else:
        out_shape = [
            jax.ShapeDtypeStruct((heads * HEAD, queries), jnp.float32),
            jax.ShapeDtypeStruct((heads * 8, queries), jnp.float32),
        ]
        out_specs = state_specs
    n = sum(b.shape[0] // 2 for b in kv_blocks)
    return pl.pallas_call(
        functools.partial(flash_kernel, first, last, len(kv_blocks)),
        grid=(heads,),
        out_shape=out_shape,
        in_specs=in_specs + ([] if first else state_specs),
        out_specs=out_specs,
        compiler_params=params(),
        cost_estimate=cost(4 * heads * queries * n * HEAD * 2, 4e6, heads * queries * n),
        name="flash",
    )(*q_parts, *kv_blocks, *(state or ()))


def merge_kernel(*refs):
    msgs, outs = refs[:NX], refs[NX:]
    lse = [jnp.sum(m[HEAD : HEAD + 16, :].astype(jnp.float32), axis=0, keepdims=True) for m in msgs]
    top = functools.reduce(jnp.maximum, lse)
    weight = [jnp.exp2(v - top) for v in lse]
    scale = 1.0 / functools.reduce(jnp.add, weight)
    o = functools.reduce(
        jnp.add, [(w * scale) * m[:HEAD, :].astype(jnp.float32) for w, m in zip(weight, msgs)]
    )
    o = o.T.astype(jnp.bfloat16)
    for i, out in enumerate(outs):
        out[...] = o[i * TOK : (i + 1) * TOK, :]


def merge(msgs):
    heads = msgs[0].shape[1] // HEAD
    return pl.pallas_call(
        merge_kernel,
        grid=(heads,),
        out_shape=[jax.ShapeDtypeStruct((TOK, heads * HEAD), jnp.bfloat16)] * NY,
        in_specs=[pl.BlockSpec((HEAD + 16, HEAD), lambda h: (0, h))] * NX,
        out_specs=[pl.BlockSpec((TOK, HEAD), lambda h: (0, h))] * NY,
        compiler_params=params(),
        cost_estimate=cost(1e6, 1e6),
        name="merge",
    )(*msgs)


def assemble_kernel(where_ref, *refs):
    out = refs[-1]
    for d in range(NY):
        group = lax.rem(where_ref[0] + d, NY)
        for c in range(CHUNKS):
            at = group * (GROUP_HEADS * HEAD) + c * WIDTH
            out[:, pl.ds(pl.multiple_of(at, HEAD), WIDTH)] = refs[c * NY + d][...]


def assemble(where, pieces):
    vmem = pl.BlockSpec(memory_space=pltpu.VMEM)
    return pl.pallas_call(
        assemble_kernel,
        out_shape=jax.ShapeDtypeStruct((TOK, NY * GROUP_HEADS * HEAD), jnp.bfloat16),
        in_specs=[pl.BlockSpec(memory_space=pltpu.SMEM)] + [vmem] * len(pieces),
        out_specs=vmem,
        compiler_params=params(),
        cost_estimate=cost(1e5, 4e5),
        name="assemble",
    )(where, *pieces)


def on_device(
    queries, keys_edit, values_edit, keys_source, values_source, edit_mask, inject_gate, step_index
):
    seq, uly = lax.axis_index("seq"), lax.axis_index("ulysses")
    y = 2 * (uly // NX) + seq // (2 * NZ)
    where = jnp.stack([y, uly]).astype(jnp.int32)
    sent = mix(
        where, step_index, queries, keys_edit, values_edit, keys_source, values_source, edit_mask, inject_gate
    )
    pieces = [None] * (CHUNKS * NY)
    for c in range(CHUNKS):
        mine = sent[c * NY : (c + 1) * NY]
        got = [mine[0]] + [shift_y(mine[d], d) for d in range(1, NY)]
        own = jnp.concatenate([g[:TOK] for g in got] + [g[TOK : 2 * TOK] for g in got], axis=0)
        query = jnp.concatenate([g[2 * TOK :] for g in got], axis=0)
        one, two = own, swap_core(own)
        q_parts = [query] + [shift_x(query, d) for d in range(1, NX)]
        state = flash(q_parts, [one, two], None, False)
        for step in range(3):
            one, two = ring_z(one), ring_z(two)
            state = flash(q_parts, [one, two, swap_core(one), swap_core(two)], state, False)
        one = ring_z(one)
        msgs = flash(q_parts, [one, swap_core(one)], state, True)
        back = [msgs[0]] + [shift_x(msgs[d], -d) for d in range(1, NX)]
        merged = merge(back)
        for d in range(NY):
            pieces[c * NY + d] = merged[0] if d == 0 else shift_y(merged[d], -d)
    return assemble(where, pieces)


def solution(mesh):
    in_specs = (
        P(("seq", "ulysses"), None),
        P(("seq", "ulysses"), None),
        P(("seq", "ulysses"), None),
        P(("seq", "ulysses"), None),
        P(("seq", "ulysses"), None),
        P("seq"),
        P(),
        P(),
    )
    out_specs = P(("seq", "ulysses"), None)
    return jax.shard_map(
        on_device, mesh=mesh, in_specs=in_specs, out_specs=out_specs, check_vma=False
    )
```

```python
import functools

import jax
import jax.numpy as jnp
from jax import lax
from jax.experimental import pallas as pl
from jax.experimental.pallas import tpu as pltpu
from jax.sharding import Mesh
from jax.sharding import PartitionSpec as P

AXES = ("yl", "z", "core", "yh", "x")
SIZES = (2, 8, 2, 2, 4)
NX, NY, NZ = 4, 4, 8
HEAD = 128
TOK = 32
HEADS = 6
WIDTH = HEADS * HEAD
TAIL = 128
LOG2E = 1.4426950408889634
SCALE2 = HEAD**-0.5 * LOG2E
VMEM_LIMIT = 32 * 1024 * 1024
BF16, F32 = jnp.bfloat16, jnp.float32
IN_VMEM = pl.BlockSpec(memory_space=pltpu.VMEM)
IN_SMEM = pl.BlockSpec(memory_space=pltpu.SMEM)


def permute(value, move):
    pairs = []
    for index in range(2 * NX * NY * NZ):
        rest, x = divmod(index, NX)
        rest, yh = divmod(rest, 2)
        rest, core = divmod(rest, 2)
        yl, z = divmod(rest, NZ)
        x, y, z, core = move(x, 2 * yh + yl, z, core)
        pairs.append((index, ((((y % 2) * NZ + z) * 2 + core) * 2 + y // 2) * NX + x))
    return lax.ppermute(value, AXES, pairs)


def shift_x(value, d):
    return permute(value, lambda x, y, z, c: ((x + d) % NX, y, z, c))


def shift_y(value, d):
    return permute(value, lambda x, y, z, c: (x, (y + d) % NY, z, c))


def ring_z(value):
    return permute(value, lambda x, y, z, c: (x, y, (z + 1 - 2 * c) % NZ, c))


def swap_core(value):
    return permute(value, lambda x, y, z, c: (x, y, z, 1 - c))


def options(us, limit=VMEM_LIMIT):
    return dict(
        compiler_params=pltpu.CompilerParams(vmem_limit_bytes=limit),
        cost_estimate=pl.CostEstimate(flops=int(us * 1.0e9), bytes_accessed=int(us * 3.0e6), transcendentals=0),
    )


def mix_kernel(where_ref, step_ref, q_hbm, ke_hbm, ve_hbm, ks_hbm, vs_hbm, mask_hbm, gate_hbm, *refs):
    sources = (mask_hbm, gate_hbm, ke_hbm, ks_hbm, ve_hbm, vs_hbm, q_hbm)
    outs, scratch, gates, sem = refs[: NY + 1], refs[NY + 1 : -2], refs[-2], refs[-1]
    copies = [pltpu.make_async_copy(a, b, sem.at[i]) for i, (a, b) in enumerate(zip(sources, scratch))]
    for copy in copies:
        copy.start()
    for copy in copies:
        copy.wait()
    mask_ref, gate_ref, ke_ref, ks_ref, ve_ref, vs_ref, q_ref = scratch
    y, u = where_ref[0], where_ref[2]
    span = mask_ref.shape[1]
    lane = lax.broadcasted_iota(jnp.int32, (TOK, span), 1)
    row = lax.broadcasted_iota(jnp.int32, (TOK, span), 0)
    picked = jnp.where(lane == u * TOK + row, jnp.broadcast_to(mask_ref[...], (TOK, span)), 0)
    inside = jnp.sum(picked, axis=1, keepdims=True) == 1
    step_lane = lax.broadcasted_iota(jnp.int32, gate_ref.shape, 1)
    at_step = jnp.sum(jnp.where(step_lane == step_ref[0], gate_ref[...], 0.0), axis=1, keepdims=True)
    gates[...] = jnp.broadcast_to(at_step, gates.shape)
    for d in range(NY):
        group = lax.rem(y + d, NY)
        for h in range(HEADS):
            head = group * HEADS + h
            strength = gates[pl.ds(head, 1), :]
            cols = pl.ds(pl.multiple_of(head * HEAD, HEAD), HEAD)
            to = slice(h * HEAD, (h + 1) * HEAD)
            for n, (edit, source) in enumerate(((ke_ref, ks_ref), (ve_ref, vs_ref))):
                e = edit[:, cols].astype(F32)
                s = source[:, cols].astype(F32)
                mixed = jnp.where(inside, e, s + strength * (e - s))
                outs[d][n * TOK : (n + 1) * TOK, to] = mixed.astype(BF16)
            if d == 0:
                outs[NY][:, to] = q_ref[:, cols]
            else:
                outs[d][2 * TOK :, to] = q_ref[:, cols]


def mix(where, step_index, queries, ke, ve, ks, vs, edit_mask, gate):
    edit_mask = edit_mask.reshape(1, -1)
    gate = gate.T
    big = pltpu.VMEM(queries.shape, BF16)
    return pl.pallas_call(
        mix_kernel,
        out_shape=[jax.ShapeDtypeStruct((n * TOK, WIDTH), BF16) for n in (2, 3, 3, 3, 1)],
        in_specs=[IN_SMEM, IN_SMEM] + [pl.BlockSpec(memory_space=pltpu.HBM)] * 7,
        out_specs=[IN_VMEM] * (NY + 1),
        scratch_shapes=[pltpu.VMEM(edit_mask.shape, jnp.int32), pltpu.VMEM(gate.shape, F32)]
        + [big] * 5
        + [pltpu.VMEM((gate.shape[0], HEAD), F32)]
        + [pltpu.SemaphoreType.DMA((7,))],
        name="mix",
        **options(2, 60 * 1024 * 1024),
    )(where, step_index, queries, ke, ve, ks, vs, edit_mask, gate)


def flash_kernel(first, last, blocks, *refs):
    refs = list(refs)
    if last:
        where_ref, refs = refs[0], refs[1:]
    q_refs, refs = refs[:NX], refs[NX:]
    kv_refs, refs = refs[:blocks], refs[blocks:]
    if not first:
        acc_in, ml_in, refs = refs[0], refs[1], refs[2:]
    rows = NY * TOK
    logs = [[] for _ in range(NX)]
    for h in range(HEADS):
        cols = slice(h * HEAD, (h + 1) * HEAD)
        pieces = [(r, at) for r in kv_refs for at in range(0, r.shape[0], 2 * TOK)]
        keys = jnp.concatenate([r[at : at + TOK, cols] for r, at in pieces], axis=0)
        values = jnp.concatenate([r[at + TOK : at + 2 * TOK, cols] for r, at in pieces], axis=0)
        for part in range(NX):
            at = slice(part * rows, (part + 1) * rows)
            q = q_refs[part][:, cols]
            s = lax.dot_general(keys, q, (((1,), (1,)), ((), ())), preferred_element_type=F32)
            top = jnp.max(s, axis=0, keepdims=True)
            if not first:
                old = ml_in[8 * h : 8 * h + 1, at]
                top = jnp.maximum(top, old)
            p = jnp.exp2((s - top) * SCALE2)
            total = jnp.sum(p, axis=0, keepdims=True)
            o = lax.dot_general(values, p.astype(BF16), (((0,), (0,)), ((), ())), preferred_element_type=F32)
            if not first:
                alpha = jnp.exp2((old - top) * SCALE2)
                total = total + alpha * ml_in[8 * h + 1 : 8 * h + 2, at]
                o = o + alpha * acc_in[cols, at]
            if last:
                o = (o * (1.0 / total)).T.astype(BF16)
                for e in range(NY):
                    out_at = pl.ds(target(where_ref, part, e) * TOK, TOK)
                    refs[0][out_at, cols] = o[e * TOK : (e + 1) * TOK, :]
                lse = top * SCALE2 + jnp.log2(total)
                hi = lse.astype(BF16).astype(F32)
                mid = (lse - hi).astype(BF16).astype(F32)
                logs[part].append((hi, mid, lse - hi - mid))
            else:
                refs[0][cols, at] = o
                refs[1][8 * h : 8 * h + 1, at] = top
                refs[1][8 * h + 1 : 8 * h + 2, at] = total
    if last:
        for part in range(NX):
            pad = jnp.zeros((TAIL - 3 * HEADS, rows), F32)
            columns = [log[i] for i in range(3) for log in logs[part]]
            packed = jnp.concatenate(columns + [pad], axis=0).T.astype(BF16)
            for e in range(NY):
                out_at = pl.ds(target(where_ref, part, e) * TOK, TOK)
                refs[0][out_at, WIDTH:] = packed[e * TOK : (e + 1) * TOK, :]


def target(where_ref, d, e):
    y = lax.rem(where_ref[0] + (NY - e), NY)
    x = lax.rem(where_ref[1] + (NX - d), NX)
    return (lax.rem(y, 2) * 2 + y // 2) * NX + x


def flash(q_parts, kv_blocks, state, where):
    queries = NX * NY * TOK
    first, last = state is None, where is not None
    if last:
        out_shape = jax.ShapeDtypeStruct((queries, WIDTH + TAIL), BF16)
    else:
        out_shape = [
            jax.ShapeDtypeStruct((WIDTH, queries), F32),
            jax.ShapeDtypeStruct((8 * HEADS, queries), F32),
        ]
    n = sum(b.shape[0] // 2 for b in kv_blocks)
    args = ([where] if last else []) + list(q_parts) + list(kv_blocks) + list(state or ())
    return pl.pallas_call(
        functools.partial(flash_kernel, first, last, len(kv_blocks)),
        out_shape=out_shape,
        in_specs=[IN_SMEM] * last + [IN_VMEM] * (len(args) - last),
        out_specs=IN_VMEM if last else [IN_VMEM, IN_VMEM],
        name="flash",
        **options(1.5 + n * 0.0045),
    )(*args)


def merge_kernel(in_ref, out_ref):
    lse = in_ref[:, WIDTH:].astype(F32)
    lse = lse[:, :HEADS] + lse[:, HEADS : 2 * HEADS] + lse[:, 2 * HEADS : 3 * HEADS]
    for y in range(NY):
        first = ((y % 2) * 2 + y // 2) * NX
        rows = [slice((first + x) * TOK, (first + x + 1) * TOK) for x in range(NX)]
        top = functools.reduce(jnp.maximum, [lse[r] for r in rows])
        weight = [jnp.exp2(lse[r] - top) for r in rows]
        scale = 1.0 / functools.reduce(jnp.add, weight)
        weight = [w * scale for w in weight]
        for h in range(HEADS):
            cols = slice(h * HEAD, (h + 1) * HEAD)
            total = functools.reduce(
                jnp.add, [w[:, h : h + 1] * in_ref[r, cols].astype(F32) for w, r in zip(weight, rows)]
            )
            at = y * WIDTH + h * HEAD
            out_ref[:, at : at + HEAD] = total.astype(BF16)


def merge(parts):
    return pl.pallas_call(
        merge_kernel,
        out_shape=jax.ShapeDtypeStruct((TOK, NY * WIDTH), BF16),
        in_specs=[IN_VMEM],
        out_specs=IN_VMEM,
        name="merge",
        **options(2),
    )(parts)


def on_device(
    queries, keys_edit, values_edit, keys_source, values_source, edit_mask, inject_gate, step_index
):
    x, y = lax.axis_index("x"), 2 * lax.axis_index("yh") + lax.axis_index("yl")
    where = jnp.stack([y, x, lax.axis_index("yh") * NX + x]).astype(jnp.int32)
    mixed = mix(
        where, step_index, queries, keys_edit, values_edit, keys_source, values_source, edit_mask, inject_gate
    )
    got = [shift_y(mixed[d], d) for d in (1, 3, 2)]
    near = jnp.concatenate([mixed[0]] + [v[: 2 * TOK] for v in got], axis=0)
    query = jnp.concatenate([mixed[NY], got[0][2 * TOK :], got[2][2 * TOK :], got[1][2 * TOK :]], axis=0)
    far = swap_core(near)
    q_parts = [query] + [shift_x(query, d) for d in range(1, NX)]
    near0, far0 = near, far
    for step in range(NZ // 2 - 1):
        near, far = ring_z(near), ring_z(far)
        if step == 0:
            near, *q_parts = lax.optimization_barrier([near, *q_parts])
            state = flash(q_parts, [near0, far0], None, None)
        state = flash(q_parts, [near, swap_core(near)], state, None)
        state = flash(q_parts, [far, swap_core(far)], state, None)
    near = ring_z(near)
    parts = flash(q_parts, [near, swap_core(near)], state, where)
    parts = lax.all_to_all(parts, ("yl", "yh", "x"), 0, 0, tiled=True)
    return merge(parts)


def solution(mesh):
    mesh = Mesh(mesh.devices.reshape(SIZES), AXES)
    tokens = P(AXES, None)
    in_specs = (tokens,) * 5 + (P(("yl", "z", "core")), P(), P())
    return jax.shard_map(on_device, mesh=mesh, in_specs=in_specs, out_specs=tokens, check_vma=False)
```

```python
import functools

import jax
import jax.numpy as jnp
from jax import lax
from jax.experimental import pallas as pl
from jax.experimental.pallas import tpu as pltpu
from jax.sharding import Mesh
from jax.sharding import PartitionSpec as P

AXES = ("yl", "z", "core", "yh", "xh", "xl")
SIZES = (2, 8, 2, 2, 2, 2)
GROUP_AXES = ("yl", "yh", "xl")
OUT_AXES = ("yl", "yh", "xh", "xl")
GROUPS, PARTS, NZ = 8, 2, 8
HEAD = 128
TOK = 32
HEADS = 3
WIDTH = HEADS * HEAD
TAIL = 128
LOG2E = 1.4426950408889634
SCALE2 = HEAD**-0.5 * LOG2E
VMEM_LIMIT = 32 * 1024 * 1024
BF16, F32 = jnp.bfloat16, jnp.float32
IN_VMEM = pl.BlockSpec(memory_space=pltpu.VMEM)
IN_SMEM = pl.BlockSpec(memory_space=pltpu.SMEM)


def ring_z(value):
    pairs = [(2 * z + c, 2 * ((z + 1 - 2 * c) % NZ) + c) for z in range(NZ) for c in range(2)]
    return lax.ppermute(value, ("z", "core"), pairs)


def swap(value, axis):
    return lax.ppermute(value, axis, [(0, 1), (1, 0)])


def options(us, limit=VMEM_LIMIT):
    return dict(
        compiler_params=pltpu.CompilerParams(vmem_limit_bytes=limit),
        cost_estimate=pl.CostEstimate(flops=int(us * 1.0e9), bytes_accessed=int(us * 3.0e6), transcendentals=0),
    )


def mix_kernel(step_ref, q_hbm, ke_hbm, ve_hbm, ks_hbm, vs_hbm, mask_hbm, gate_hbm, out, *refs):
    sources = (mask_hbm, gate_hbm, ke_hbm, ks_hbm, ve_hbm, vs_hbm, q_hbm)
    scratch, gates, sem = refs[:-2], refs[-2], refs[-1]
    copies = [pltpu.make_async_copy(a, b, sem.at[i]) for i, (a, b) in enumerate(zip(sources, scratch))]
    for copy in copies:
        copy.start()
    mask_ref, gate_ref, ke_ref, ks_ref, ve_ref, vs_ref, q_ref = scratch
    copies[0].wait()
    copies[1].wait()
    span = mask_ref.shape[1]
    uly = (lax.axis_index("yh") * 2 + lax.axis_index("xh")) * 2 + lax.axis_index("xl")
    lane = lax.broadcasted_iota(jnp.int32, (TOK, span), 1)
    row = lax.broadcasted_iota(jnp.int32, (TOK, span), 0)
    picked = jnp.where(lane == uly * TOK + row, jnp.broadcast_to(mask_ref[...], (TOK, span)), 0)
    inside = jnp.sum(picked, axis=1, keepdims=True) == 1
    step_lane = lax.broadcasted_iota(jnp.int32, gate_ref.shape, 1)
    at_step = jnp.sum(jnp.where(step_lane == step_ref[0], gate_ref[...], 0.0), axis=1, keepdims=True)
    gates[...] = jnp.broadcast_to(at_step, gates.shape)
    for n, (edit, source) in enumerate(((ke_ref, ks_ref), (ve_ref, vs_ref))):
        copies[2 + 2 * n].wait()
        copies[3 + 2 * n].wait()
        for head in range(GROUPS * HEADS):
            strength = gates[head : head + 1, :]
            cols = slice(head * HEAD, (head + 1) * HEAD)
            e = edit[:, cols].astype(F32)
            s = source[:, cols].astype(F32)
            mixed = jnp.where(inside, e, s + strength * (e - s)).astype(BF16)
            group, h = divmod(head, HEADS)
            out[group, n * TOK : (n + 1) * TOK, h * HEAD : (h + 1) * HEAD] = mixed
    copies[6].wait()
    for group in range(GROUPS):
        out[group, 2 * TOK :, :] = q_ref[:, group * WIDTH : (group + 1) * WIDTH]


def mix(step_index, queries, ke, ve, ks, vs, edit_mask, gate):
    edit_mask = edit_mask.reshape(1, -1)
    gate = gate.T
    big = pltpu.VMEM(queries.shape, BF16)
    return pl.pallas_call(
        mix_kernel,
        out_shape=jax.ShapeDtypeStruct((GROUPS, 3 * TOK, WIDTH), BF16),
        in_specs=[IN_SMEM] + [pl.BlockSpec(memory_space=pltpu.HBM)] * 7,
        out_specs=IN_VMEM,
        scratch_shapes=[pltpu.VMEM(edit_mask.shape, jnp.int32), pltpu.VMEM(gate.shape, F32)]
        + [big] * 5
        + [pltpu.VMEM((gate.shape[0], HEAD), F32)]
        + [pltpu.SemaphoreType.DMA((7,))],
        name="mix",
        **options(2, 60 * 1024 * 1024),
    )(step_index, queries, ke, ve, ks, vs, edit_mask, gate)


def flash_kernel(first, last, blocks, *refs):
    refs = list(refs)
    q_refs, refs = refs[:PARTS], refs[PARTS:]
    kv_refs, refs = refs[:blocks], refs[blocks:]
    if not first:
        acc_in, ml_in, refs = refs[0], refs[1], refs[2:]
    tile = 4 * TOK
    tiles = GROUPS // 4
    logs = [[] for _ in range(PARTS * tiles)]
    for h in range(HEADS):
        cols = slice(h * HEAD, (h + 1) * HEAD)
        pieces = [(r, at) for r in kv_refs for at in range(0, r.shape[0], 2 * TOK)]
        keys = jnp.concatenate([r[at : at + TOK, cols] for r, at in pieces], axis=0)
        values = jnp.concatenate([r[at + TOK : at + 2 * TOK, cols] for r, at in pieces], axis=0)
        for part in range(PARTS * tiles):
            at = slice(part * tile, (part + 1) * tile)
            begin = part % tiles * tile
            q = q_refs[part // tiles][begin : begin + tile, cols]
            s = lax.dot_general(keys, q, (((1,), (1,)), ((), ())), preferred_element_type=F32)
            top = jnp.max(s, axis=0, keepdims=True)
            if not first:
                old = ml_in[8 * h : 8 * h + 1, at]
                top = jnp.maximum(top, old)
            p = jnp.exp2((s - top) * SCALE2)
            total = jnp.sum(p, axis=0, keepdims=True)
            o = lax.dot_general(values, p.astype(BF16), (((0,), (0,)), ((), ())), preferred_element_type=F32)
            if not first:
                alpha = jnp.exp2((old - top) * SCALE2)
                total = total + alpha * ml_in[8 * h + 1 : 8 * h + 2, at]
                o = o + alpha * acc_in[cols, at]
            if last:
                o = (o * (1.0 / total)).T.astype(BF16)
                for e in range(4):
                    refs[0][target(part, e), cols] = o[e * TOK : (e + 1) * TOK, :]
                lse = top * SCALE2 + jnp.log2(total)
                hi = lse.astype(BF16).astype(F32)
                mid = (lse - hi).astype(BF16).astype(F32)
                logs[part].append((hi, mid, lse - hi - mid))
            else:
                refs[0][cols, at] = o
                refs[1][8 * h : 8 * h + 1, at] = top
                refs[1][8 * h + 1 : 8 * h + 2, at] = total
    if last:
        for part in range(PARTS * tiles):
            pad = jnp.zeros((TAIL - 3 * HEADS, tile), F32)
            columns = [log[i] for i in range(3) for log in logs[part]]
            packed = jnp.concatenate(columns + [pad], axis=0).T.astype(BF16)
            for e in range(4):
                refs[0][target(part, e), WIDTH:] = packed[e * TOK : (e + 1) * TOK, :]


def target(part, e):
    source = part % (GROUPS // 4) * 4 + e
    xh = lax.axis_index("xh")
    xh = xh if part < GROUPS // 4 else 1 - xh
    return pl.ds(((source // 2 * 2 + xh) * 2 + source % 2) * TOK, TOK)


def flash(q_parts, kv_blocks, state, last=False):
    queries = PARTS * GROUPS * TOK
    first = state is None
    if last:
        out_shape = jax.ShapeDtypeStruct((queries, WIDTH + TAIL), BF16)
    else:
        out_shape = [
            jax.ShapeDtypeStruct((WIDTH, queries), F32),
            jax.ShapeDtypeStruct((8 * HEADS, queries), F32),
        ]
    n = sum(b.shape[0] // 2 for b in kv_blocks)
    args = list(q_parts) + list(kv_blocks) + list(state or ())
    return pl.pallas_call(
        functools.partial(flash_kernel, first, last, len(kv_blocks)),
        out_shape=out_shape,
        in_specs=[IN_VMEM] * len(args),
        out_specs=IN_VMEM if last else [IN_VMEM, IN_VMEM],
        name="flash",
        **options(1 + n * 0.0023),
    )(*args)


def merge_kernel(in_ref, out_ref):
    lse = in_ref[:, WIDTH:].astype(F32)
    lse = lse[:, :HEADS] + lse[:, HEADS : 2 * HEADS] + lse[:, 2 * HEADS : 3 * HEADS]
    for group in range(GROUPS):
        first = group // 2 * 4 + group % 2
        rows = [slice(r * TOK, (r + 1) * TOK) for r in (first, first + 2)]
        top = jnp.maximum(lse[rows[0]], lse[rows[1]])
        weight = [jnp.exp2(lse[r] - top) for r in rows]
        scale = 1.0 / (weight[0] + weight[1])
        weight = [w * scale for w in weight]
        for h in range(HEADS):
            cols = slice(h * HEAD, (h + 1) * HEAD)
            total = functools.reduce(
                jnp.add, [w[:, h : h + 1] * in_ref[r, cols].astype(F32) for w, r in zip(weight, rows)]
            )
            at = group * WIDTH + h * HEAD
            out_ref[:, at : at + HEAD] = total.astype(BF16)


def merge(parts):
    return pl.pallas_call(
        merge_kernel,
        out_shape=jax.ShapeDtypeStruct((TOK, GROUPS * WIDTH), BF16),
        in_specs=[IN_VMEM],
        out_specs=IN_VMEM,
        name="merge",
        **options(2),
    )(parts)


def on_device(
    queries, keys_edit, values_edit, keys_source, values_source, edit_mask, inject_gate, step_index
):
    mixed = mix(
        step_index, queries, keys_edit, values_edit, keys_source, values_source, edit_mask, inject_gate
    )
    got = lax.all_to_all(mixed, GROUP_AXES, 0, 0, tiled=True)
    near = got[:, : 2 * TOK].reshape(-1, WIDTH)
    query = got[:, 2 * TOK :].reshape(-1, WIDTH)
    far = swap(near, "core")
    q_parts = [query, swap(query, "xh")]
    state = flash(q_parts, [near, far], None)
    for step in range(NZ // 2 - 1):
        near, far = ring_z(near), ring_z(far)
        state = flash(q_parts, [near, swap(near, "core")], state)
        state = flash(q_parts, [far, swap(far, "core")], state)
    near = ring_z(near)
    parts = flash(q_parts, [near, swap(near, "core")], state, last=True)
    parts = lax.all_to_all(parts, OUT_AXES, 0, 0, tiled=True)
    return merge(parts)


def solution(mesh):
    mesh = Mesh(mesh.devices.reshape(SIZES), AXES)
    tokens = P(AXES, None)
    in_specs = (tokens,) * 5 + (P(("yl", "z", "core")), P(), P())
    return jax.shard_map(on_device, mesh=mesh, in_specs=in_specs, out_specs=tokens, check_vma=False)
```

```python
import functools

import jax
import jax.numpy as jnp
from jax import lax
from jax.experimental import pallas as pl
from jax.experimental.pallas import tpu as pltpu
from jax.sharding import Mesh
from jax.sharding import PartitionSpec as P

AXES = ("yl", "z", "core", "yh", "xh", "xl")
SIZES = (2, 8, 2, 2, 2, 2)
GROUP_AXES = ("yl", "yh", "xh")
OUT_AXES = ("yl", "yh", "xl", "xh")
GROUPS, PARTS, NZ = 8, 2, 8
HEAD = 128
TOK = 32
HEADS = 3
WIDTH = HEADS * HEAD
TAIL = 128
LOG2E = 1.4426950408889634
SCALE2 = HEAD**-0.5 * LOG2E
VMEM_LIMIT = 32 * 1024 * 1024
BF16, F32 = jnp.bfloat16, jnp.float32
IN_VMEM = pl.BlockSpec(memory_space=pltpu.VMEM)
IN_SMEM = pl.BlockSpec(memory_space=pltpu.SMEM)


def ring_z(value):
    pairs = [(2 * z + c, 2 * ((z + 1 - 2 * c) % NZ) + c) for z in range(NZ) for c in range(2)]
    return lax.ppermute(value, ("z", "core"), pairs)


def swap(value, axis):
    return lax.ppermute(value, axis, [(0, 1), (1, 0)])


def options(us, limit=VMEM_LIMIT):
    return dict(
        compiler_params=pltpu.CompilerParams(vmem_limit_bytes=limit),
        cost_estimate=pl.CostEstimate(flops=int(us * 1.0e9), bytes_accessed=int(us * 3.0e6), transcendentals=0),
    )


def mix_kernel(step_ref, q_hbm, ke_hbm, ve_hbm, ks_hbm, vs_hbm, mask_hbm, gate_hbm, out, *refs):
    sources = (mask_hbm, gate_hbm, ke_hbm, ks_hbm, ve_hbm, vs_hbm, q_hbm)
    scratch, gates, sem = refs[:-2], refs[-2], refs[-1]
    copies = [pltpu.make_async_copy(a, b, sem.at[i]) for i, (a, b) in enumerate(zip(sources, scratch))]
    for copy in copies:
        copy.start()
    mask_ref, gate_ref, ke_ref, ks_ref, ve_ref, vs_ref, q_ref = scratch
    copies[0].wait()
    copies[1].wait()
    span = mask_ref.shape[1]
    uly = (lax.axis_index("yh") * 2 + lax.axis_index("xh")) * 2 + lax.axis_index("xl")
    lane = lax.broadcasted_iota(jnp.int32, (TOK, span), 1)
    row = lax.broadcasted_iota(jnp.int32, (TOK, span), 0)
    picked = jnp.where(lane == uly * TOK + row, jnp.broadcast_to(mask_ref[...], (TOK, span)), 0)
    inside = jnp.sum(picked, axis=1, keepdims=True) == 1
    step_lane = lax.broadcasted_iota(jnp.int32, gate_ref.shape, 1)
    at_step = jnp.sum(jnp.where(step_lane == step_ref[0], gate_ref[...], 0.0), axis=1, keepdims=True)
    gates[...] = jnp.broadcast_to(at_step, gates.shape)
    for n, (edit, source) in enumerate(((ke_ref, ks_ref), (ve_ref, vs_ref))):
        copies[2 + 2 * n].wait()
        copies[3 + 2 * n].wait()
        for head in range(GROUPS * HEADS):
            strength = gates[head : head + 1, :]
            cols = slice(head * HEAD, (head + 1) * HEAD)
            e = edit[:, cols].astype(F32)
            s = source[:, cols].astype(F32)
            mixed = jnp.where(inside, e, s + strength * (e - s)).astype(BF16)
            group, h = divmod(head, HEADS)
            out[group, n * TOK : (n + 1) * TOK, h * HEAD : (h + 1) * HEAD] = mixed
    copies[6].wait()
    for group in range(GROUPS):
        out[group, 2 * TOK :, :] = q_ref[:, group * WIDTH : (group + 1) * WIDTH]


def mix(step_index, queries, ke, ve, ks, vs, edit_mask, gate):
    edit_mask = edit_mask.reshape(1, -1)
    gate = gate.T
    big = pltpu.VMEM(queries.shape, BF16)
    return pl.pallas_call(
        mix_kernel,
        out_shape=jax.ShapeDtypeStruct((GROUPS, 3 * TOK, WIDTH), BF16),
        in_specs=[IN_SMEM] + [pl.BlockSpec(memory_space=pltpu.HBM)] * 7,
        out_specs=IN_VMEM,
        scratch_shapes=[pltpu.VMEM(edit_mask.shape, jnp.int32), pltpu.VMEM(gate.shape, F32)]
        + [big] * 5
        + [pltpu.VMEM((gate.shape[0], HEAD), F32)]
        + [pltpu.SemaphoreType.DMA((7,))],
        name="mix",
        **options(2, 60 * 1024 * 1024),
    )(step_index, queries, ke, ve, ks, vs, edit_mask, gate)


def flash_kernel(first, last, blocks, *refs):
    refs = list(refs)
    q_refs, refs = refs[:PARTS], refs[PARTS:]
    kv_refs, refs = refs[:blocks], refs[blocks:]
    if not first:
        acc_in, ml_in, refs = refs[0], refs[1], refs[2:]
    tile = 4 * TOK
    tiles = GROUPS // 4
    logs = [[] for _ in range(PARTS * tiles)]
    for h in range(HEADS):
        cols = slice(h * HEAD, (h + 1) * HEAD)
        pieces = [(r, at) for r in kv_refs for at in range(0, r.shape[0], 2 * TOK)]
        keys = jnp.concatenate([r[at : at + TOK, cols] for r, at in pieces], axis=0)
        values = jnp.concatenate([r[at + TOK : at + 2 * TOK, cols] for r, at in pieces], axis=0)
        for part in range(PARTS * tiles):
            at = slice(part * tile, (part + 1) * tile)
            begin = part % tiles * tile
            q = q_refs[part // tiles][begin : begin + tile, cols]
            s = lax.dot_general(keys, q, (((1,), (1,)), ((), ())), preferred_element_type=F32)
            top = jnp.max(s, axis=0, keepdims=True)
            if not first:
                old = ml_in[8 * h : 8 * h + 1, at]
                top = jnp.maximum(top, old)
            p = jnp.exp2((s - top) * SCALE2)
            total = jnp.sum(p, axis=0, keepdims=True)
            o = lax.dot_general(values, p.astype(BF16), (((0,), (0,)), ((), ())), preferred_element_type=F32)
            if not first:
                alpha = jnp.exp2((old - top) * SCALE2)
                total = total + alpha * ml_in[8 * h + 1 : 8 * h + 2, at]
                o = o + alpha * acc_in[cols, at]
            if last:
                o = (o * (1.0 / total)).T.astype(BF16)
                for e in range(4):
                    refs[0][target(part, e), cols] = o[e * TOK : (e + 1) * TOK, :]
                lse = top * SCALE2 + jnp.log2(total)
                hi = lse.astype(BF16).astype(F32)
                mid = (lse - hi).astype(BF16).astype(F32)
                logs[part].append((hi, mid, lse - hi - mid))
            else:
                refs[0][cols, at] = o
                refs[1][8 * h : 8 * h + 1, at] = top
                refs[1][8 * h + 1 : 8 * h + 2, at] = total
    if last:
        for part in range(PARTS * tiles):
            pad = jnp.zeros((TAIL - 3 * HEADS, tile), F32)
            columns = [log[i] for i in range(3) for log in logs[part]]
            packed = jnp.concatenate(columns + [pad], axis=0).T.astype(BF16)
            for e in range(4):
                refs[0][target(part, e), WIDTH:] = packed[e * TOK : (e + 1) * TOK, :]


def target(part, e):
    source = part % (GROUPS // 4) * 4 + e
    xh = lax.axis_index("xl")
    xh = xh if part < GROUPS // 4 else 1 - xh
    return pl.ds(((source // 2 * 2 + xh) * 2 + source % 2) * TOK, TOK)


def flash(q_parts, kv_blocks, state, last=False):
    queries = PARTS * GROUPS * TOK
    first = state is None
    if last:
        out_shape = jax.ShapeDtypeStruct((queries, WIDTH + TAIL), BF16)
    else:
        out_shape = [
            jax.ShapeDtypeStruct((WIDTH, queries), F32),
            jax.ShapeDtypeStruct((8 * HEADS, queries), F32),
        ]
    n = sum(b.shape[0] // 2 for b in kv_blocks)
    args = list(q_parts) + list(kv_blocks) + list(state or ())
    return pl.pallas_call(
        functools.partial(flash_kernel, first, last, len(kv_blocks)),
        out_shape=out_shape,
        in_specs=[IN_VMEM] * len(args),
        out_specs=IN_VMEM if last else [IN_VMEM, IN_VMEM],
        name="flash",
        **options(1 + n * 0.0023),
    )(*args)


def attend(q_parts, block, state, last=False):
    return flash(q_parts, [block, swap(block, "core")], state, last)


def merge_kernel(in_ref, out_ref):
    lse = in_ref[:, WIDTH:].astype(F32)
    lse = lse[:, :HEADS] + lse[:, HEADS : 2 * HEADS] + lse[:, 2 * HEADS : 3 * HEADS]
    for group in range(GROUPS):
        first = group // 2 * 4 + group % 2
        rows = [slice(r * TOK, (r + 1) * TOK) for r in (first, first + 2)]
        top = jnp.maximum(lse[rows[0]], lse[rows[1]])
        weight = [jnp.exp2(lse[r] - top) for r in rows]
        scale = 1.0 / (weight[0] + weight[1])
        weight = [w * scale for w in weight]
        for h in range(HEADS):
            cols = slice(h * HEAD, (h + 1) * HEAD)
            total = functools.reduce(
                jnp.add, [w[:, h : h + 1] * in_ref[r, cols].astype(F32) for w, r in zip(weight, rows)]
            )
            at = group * WIDTH + h * HEAD
            out_ref[:, at : at + HEAD] = total.astype(BF16)


def merge(parts):
    return pl.pallas_call(
        merge_kernel,
        out_shape=jax.ShapeDtypeStruct((TOK, GROUPS * WIDTH), BF16),
        in_specs=[IN_VMEM],
        out_specs=IN_VMEM,
        name="merge",
        **options(2),
    )(parts)


def on_device(
    queries, keys_edit, values_edit, keys_source, values_source, edit_mask, inject_gate, step_index
):
    mixed = mix(
        step_index, queries, keys_edit, values_edit, keys_source, values_source, edit_mask, inject_gate
    )
    got = lax.all_to_all(mixed, GROUP_AXES, 0, 0, tiled=True)
    near = got[:, : 2 * TOK].reshape(-1, WIDTH)
    query = got[:, 2 * TOK :].reshape(-1, WIDTH)
    far = swap(near, "core")
    q_parts = [query, swap(query, "xl")]
    near1, far1 = ring_z(near), ring_z(far)
    near1, *q_parts = lax.optimization_barrier([near1, *q_parts])
    state = flash(q_parts, [near, far], None)
    near2 = ring_z(near1)
    far1, *state = lax.optimization_barrier([far1, *state])
    far2 = ring_z(far1)
    state = attend(q_parts, near1, state)
    state = attend(q_parts, far1, state)
    near3, far3 = ring_z(near2), ring_z(far2)
    state = attend(q_parts, near2, state)
    state = attend(q_parts, far2, state)
    near4 = ring_z(near3)
    state = attend(q_parts, near3, state)
    far3, *state = lax.optimization_barrier([far3, *state])
    state = attend(q_parts, far3, state)
    parts = attend(q_parts, near4, state, last=True)
    parts = lax.all_to_all(parts, OUT_AXES, 0, 0, tiled=True)
    return merge(parts)


def solution(mesh):
    mesh = Mesh(mesh.devices.reshape(SIZES), AXES)
    tokens = P(AXES, None)
    in_specs = (tokens,) * 5 + (P(("yl", "z", "core")), P(), P())
    return jax.shard_map(on_device, mesh=mesh, in_specs=in_specs, out_specs=tokens, check_vma=False)
```

```python
import functools

import jax
import jax.numpy as jnp
from jax import lax
from jax.experimental import pallas as pl
from jax.experimental.pallas import tpu as pltpu
from jax.sharding import Mesh
from jax.sharding import PartitionSpec as P

AXES = ("yl", "z", "core", "yh", "xh", "xl")
SIZES = (2, 8, 2, 2, 2, 2)
GROUP_AXES = ("yl", "yh", "xh")
OUT_AXES = ("yl", "yh", "xl", "xh")
GROUPS, PARTS, NZ = 8, 2, 8
HEAD = 128
TOK = 32
HEADS = 3
WIDTH = HEADS * HEAD
TAIL = 128
LOG2E = 1.4426950408889634
SCALE2 = HEAD**-0.5 * LOG2E
VMEM_LIMIT = 32 * 1024 * 1024
BF16, F32 = jnp.bfloat16, jnp.float32
IN_VMEM = pl.BlockSpec(memory_space=pltpu.VMEM)
IN_SMEM = pl.BlockSpec(memory_space=pltpu.SMEM)


def ring_z(value):
    pairs = [(2 * z + c, 2 * ((z + 1 - 2 * c) % NZ) + c) for z in range(NZ) for c in range(2)]
    return lax.ppermute(value, ("z", "core"), pairs)


def swap(value, axis):
    return lax.ppermute(value, axis, [(0, 1), (1, 0)])


def options(us, limit=VMEM_LIMIT):
    return dict(
        compiler_params=pltpu.CompilerParams(vmem_limit_bytes=limit),
        cost_estimate=pl.CostEstimate(flops=int(us * 1.0e9), bytes_accessed=int(us * 3.0e6), transcendentals=0),
    )


def mix_kernel(step_ref, q_hbm, ke_hbm, ve_hbm, ks_hbm, vs_hbm, mask_hbm, gate_hbm, out_hbm, *refs):
    sources = (mask_hbm, gate_hbm, ke_hbm, ks_hbm, ve_hbm, vs_hbm, q_hbm)
    scratch, gates, out, sem, out_sem = refs[:-4], refs[-4], refs[-3], refs[-2], refs[-1]
    sends = []
    copies = [pltpu.make_async_copy(a, b, sem.at[i]) for i, (a, b) in enumerate(zip(sources, scratch))]
    for copy in copies:
        copy.start()
    mask_ref, gate_ref, ke_ref, ks_ref, ve_ref, vs_ref, q_ref = scratch
    copies[0].wait()
    copies[1].wait()
    span = mask_ref.shape[1]
    uly = (lax.axis_index("yh") * 2 + lax.axis_index("xh")) * 2 + lax.axis_index("xl")
    lane = lax.broadcasted_iota(jnp.int32, (TOK, span), 1)
    row = lax.broadcasted_iota(jnp.int32, (TOK, span), 0)
    picked = jnp.where(lane == uly * TOK + row, jnp.broadcast_to(mask_ref[...], (TOK, span)), 0)
    inside = jnp.sum(picked, axis=1, keepdims=True) == 1
    step_lane = lax.broadcasted_iota(jnp.int32, gate_ref.shape, 1)
    at_step = jnp.sum(jnp.where(step_lane == step_ref[0], gate_ref[...], 0.0), axis=1, keepdims=True)
    gates[...] = jnp.broadcast_to(at_step, gates.shape)
    for n, (edit, source) in enumerate(((ke_ref, ks_ref), (ve_ref, vs_ref))):
        copies[2 + 2 * n].wait()
        copies[3 + 2 * n].wait()
        for head in range(GROUPS * HEADS):
            strength = gates[head : head + 1, :]
            cols = slice(head * HEAD, (head + 1) * HEAD)
            e = edit[:, cols].astype(F32)
            s = source[:, cols].astype(F32)
            mixed = jnp.where(inside, e, s + strength * (e - s)).astype(BF16)
            group, h = divmod(head, HEADS)
            out[group, n * TOK : (n + 1) * TOK, h * HEAD : (h + 1) * HEAD] = mixed
        rows = pl.ds(n * TOK, TOK)
        sends.append(pltpu.make_async_copy(out.at[:, rows, :], out_hbm.at[:, rows, :], out_sem.at[n]))
        sends[-1].start()
    copies[6].wait()
    for group in range(GROUPS):
        out[group, 2 * TOK :, :] = q_ref[:, group * WIDTH : (group + 1) * WIDTH]
    rows = pl.ds(2 * TOK, TOK)
    sends.append(pltpu.make_async_copy(out.at[:, rows, :], out_hbm.at[:, rows, :], out_sem.at[2]))
    sends[-1].start()
    for send in sends:
        send.wait()


def mix(step_index, queries, ke, ve, ks, vs, edit_mask, gate):
    edit_mask = edit_mask.reshape(1, -1)
    gate = gate.T
    big = pltpu.VMEM(queries.shape, BF16)
    return pl.pallas_call(
        mix_kernel,
        out_shape=jax.ShapeDtypeStruct((GROUPS, 3 * TOK, WIDTH), BF16),
        in_specs=[IN_SMEM] + [pl.BlockSpec(memory_space=pltpu.HBM)] * 7,
        out_specs=pl.BlockSpec(memory_space=pltpu.HBM),
        scratch_shapes=[pltpu.VMEM(edit_mask.shape, jnp.int32), pltpu.VMEM(gate.shape, F32)]
        + [big] * 5
        + [pltpu.VMEM((gate.shape[0], HEAD), F32)]
        + [pltpu.VMEM((GROUPS, 3 * TOK, WIDTH), BF16)]
        + [pltpu.SemaphoreType.DMA((7,)), pltpu.SemaphoreType.DMA((3,))],
        name="mix",
        **options(2, 60 * 1024 * 1024),
    )(step_index, queries, ke, ve, ks, vs, edit_mask, gate)


def flash_kernel(first, last, blocks, *refs):
    refs = list(refs)
    q_refs, refs = refs[:PARTS], refs[PARTS:]
    kv_refs, refs = refs[:blocks], refs[blocks:]
    if not first:
        acc_in, ml_in, refs = refs[0], refs[1], refs[2:]
    tile = 4 * TOK
    tiles = GROUPS // 4
    logs = [[] for _ in range(PARTS * tiles)]
    for h in range(HEADS):
        cols = slice(h * HEAD, (h + 1) * HEAD)
        pieces = [(r, at) for r in kv_refs for at in range(0, r.shape[0], 2 * TOK)]
        keys = jnp.concatenate([r[at : at + TOK, cols] for r, at in pieces], axis=0)
        values = jnp.concatenate([r[at + TOK : at + 2 * TOK, cols] for r, at in pieces], axis=0)
        for part in range(PARTS * tiles):
            at = slice(part * tile, (part + 1) * tile)
            begin = part % tiles * tile
            q = q_refs[part // tiles][begin : begin + tile, cols]
            s = lax.dot_general(keys, q, (((1,), (1,)), ((), ())), preferred_element_type=F32)
            top = jnp.max(s, axis=0, keepdims=True)
            if not first:
                old = ml_in[8 * h : 8 * h + 1, at]
                top = jnp.maximum(top, old)
            p = jnp.exp2((s - top) * SCALE2)
            total = jnp.sum(p, axis=0, keepdims=True)
            o = lax.dot_general(values, p.astype(BF16), (((0,), (0,)), ((), ())), preferred_element_type=F32)
            if not first:
                alpha = jnp.exp2((old - top) * SCALE2)
                total = total + alpha * ml_in[8 * h + 1 : 8 * h + 2, at]
                o = o + alpha * acc_in[cols, at]
            if last:
                o = (o * (1.0 / total)).T.astype(BF16)
                for e in range(4):
                    refs[0][target(part, e), cols] = o[e * TOK : (e + 1) * TOK, :]
                lse = top * SCALE2 + jnp.log2(total)
                hi = lse.astype(BF16).astype(F32)
                mid = (lse - hi).astype(BF16).astype(F32)
                logs[part].append((hi, mid, lse - hi - mid))
            else:
                refs[0][cols, at] = o
                refs[1][8 * h : 8 * h + 1, at] = top
                refs[1][8 * h + 1 : 8 * h + 2, at] = total
    if last:
        for part in range(PARTS * tiles):
            pad = jnp.zeros((TAIL - 3 * HEADS, tile), F32)
            columns = [log[i] for i in range(3) for log in logs[part]]
            packed = jnp.concatenate(columns + [pad], axis=0).T.astype(BF16)
            for e in range(4):
                refs[0][target(part, e), WIDTH:] = packed[e * TOK : (e + 1) * TOK, :]


def target(part, e):
    source = part % (GROUPS // 4) * 4 + e
    xh = lax.axis_index("xl")
    xh = xh if part < GROUPS // 4 else 1 - xh
    return pl.ds(((source // 2 * 2 + xh) * 2 + source % 2) * TOK, TOK)


def flash(q_parts, kv_blocks, state, last=False):
    queries = PARTS * GROUPS * TOK
    first = state is None
    if last:
        out_shape = jax.ShapeDtypeStruct((queries, WIDTH + TAIL), BF16)
    else:
        out_shape = [
            jax.ShapeDtypeStruct((WIDTH, queries), F32),
            jax.ShapeDtypeStruct((8 * HEADS, queries), F32),
        ]
    n = sum(b.shape[0] // 2 for b in kv_blocks)
    args = list(q_parts) + list(kv_blocks) + list(state or ())
    return pl.pallas_call(
        functools.partial(flash_kernel, first, last, len(kv_blocks)),
        out_shape=out_shape,
        in_specs=[IN_VMEM] * len(args),
        out_specs=IN_VMEM if last else [IN_VMEM, IN_VMEM],
        name="flash",
        **options(1 + n * 0.0023),
    )(*args)


def attend(q_parts, block, state, last=False):
    return flash(q_parts, [block, swap(block, "core")], state, last)


def merge_kernel(in_ref, out_ref):
    lse = in_ref[:, WIDTH:].astype(F32)
    lse = lse[:, :HEADS] + lse[:, HEADS : 2 * HEADS] + lse[:, 2 * HEADS : 3 * HEADS]
    for group in range(GROUPS):
        first = group // 2 * 4 + group % 2
        rows = [slice(r * TOK, (r + 1) * TOK) for r in (first, first + 2)]
        top = jnp.maximum(lse[rows[0]], lse[rows[1]])
        weight = [jnp.exp2(lse[r] - top) for r in rows]
        scale = 1.0 / (weight[0] + weight[1])
        weight = [w * scale for w in weight]
        for h in range(HEADS):
            cols = slice(h * HEAD, (h + 1) * HEAD)
            total = functools.reduce(
                jnp.add, [w[:, h : h + 1] * in_ref[r, cols].astype(F32) for w, r in zip(weight, rows)]
            )
            at = group * WIDTH + h * HEAD
            out_ref[:, at : at + HEAD] = total.astype(BF16)


def merge(parts):
    return pl.pallas_call(
        merge_kernel,
        out_shape=jax.ShapeDtypeStruct((TOK, GROUPS * WIDTH), BF16),
        in_specs=[IN_VMEM],
        out_specs=IN_VMEM,
        name="merge",
        **options(2),
    )(parts)


def on_device(
    queries, keys_edit, values_edit, keys_source, values_source, edit_mask, inject_gate, step_index
):
    mixed = mix(
        step_index, queries, keys_edit, values_edit, keys_source, values_source, edit_mask, inject_gate
    )
    got = lax.all_to_all(mixed, GROUP_AXES, 0, 0, tiled=True)
    near = got[:, : 2 * TOK].reshape(-1, WIDTH)
    query = got[:, 2 * TOK :].reshape(-1, WIDTH)
    far = swap(near, "core")
    q_parts = [query, swap(query, "xl")]
    near1, far1 = ring_z(near), ring_z(far)
    near1, *q_parts = lax.optimization_barrier([near1, *q_parts])
    state = flash(q_parts, [near, far], None)
    near2 = ring_z(near1)
    far1, *state = lax.optimization_barrier([far1, *state])
    far2 = ring_z(far1)
    state = attend(q_parts, near1, state)
    state = attend(q_parts, far1, state)
    near3, far3 = ring_z(near2), ring_z(far2)
    state = attend(q_parts, near2, state)
    state = attend(q_parts, far2, state)
    near4 = ring_z(near3)
    state = attend(q_parts, near3, state)
    far3, *state = lax.optimization_barrier([far3, *state])
    state = attend(q_parts, far3, state)
    parts = attend(q_parts, near4, state, last=True)
    parts = lax.all_to_all(parts, OUT_AXES, 0, 0, tiled=True)
    return merge(parts)


def solution(mesh):
    mesh = Mesh(mesh.devices.reshape(SIZES), AXES)
    tokens = P(AXES, None)
    in_specs = (tokens,) * 5 + (P(("yl", "z", "core")), P(), P())
    return jax.shard_map(on_device, mesh=mesh, in_specs=in_specs, out_specs=tokens, check_vma=False)
```
